1024 devices in a mesh: row: 64 (over z, y_lo, core), col: 16 (over x, y_hi).
Axes of the slice: x: 4, y: 8 (y_hi: 4, y_lo: 2; y = y_hi * 2 + y_lo), z: 16, core: 2. Of those that a mesh axis runs over, the one named last changes fastest.
Arguments:
- adjacency: bfloat16 [32768, 16384], P('row', 'col'), may hold values from -0.0625 to 0.0625
- block_mask: int32 [128, 64], P('row', 'col'), may hold values 0 or 1
- features: bfloat16 [16384, 512], P(('col', 'row')), may hold values from -6 to 6
- weight: bfloat16 [512, 512], replicated, may hold values from -0.25 to 0.25
- upstream: bfloat16 [32768, 512], P(('row', 'col')), may hold values from -18 to 18
Outputs:
- output: bfloat16 [32768, 512], P(('row', 'col'))
- feature_grad: float32 [16384, 512], P(('col', 'row'))
- weight_grad: float32 [512, 512], replicated
The draws below stay inside these ranges and needn't reach their ends.
All inputs are finite; a program needn't handle non-finite values. No bound on the sum of `block_mask` on one device may be relied on, other than what follows from the above.
Results may differ from the reference program's by a relative error of at most 0.011.
Values may be sent and summed in bfloat16 or wider, within the bound.
No kernel may reach another device: no remote copies, remote signals or barrier semaphores. Data moves between devices by JAX's collectives and lax.ppermute only.
A program may use at most 32 MiB of HBM per device.

```python
import jax
import jax.numpy as jnp
from jax import lax

F = 512
TILE = 256
PANEL_ROWS = 512
ROWS = 32768
COLS = 16384
N_ROW = 64
N_COL = 16


def draw_upstream(key, part):
    key = jax.random.fold_in(key, 7)
    key_base, key_cols, key_signs = jax.random.split(key, 3)
    base = jnp.clip(jax.random.normal(key_base, (ROWS, F), jnp.float32), -6.0, 6.0)
    groups = N_ROW * N_COL
    per_group = ROWS // groups
    columns = jax.random.randint(key_cols, (groups,), 0, F)
    signs = (jax.random.randint(key_signs, (groups,), 0, 2) * 2 - 1).astype(jnp.float32)
    heavy = (jnp.arange(F)[None, :] == columns[:, None]).astype(jnp.float32) * (signs[:, None] * 12.0)
    return (base + jnp.repeat(heavy, per_group, 0)).astype(jnp.bfloat16)


def with_ends(drawn, own_key, smallest, largest):
    place = [jax.random.randint(jax.random.fold_in(own_key, axis), (), 0, length) for axis, length in enumerate(drawn.shape)]
    main_axis = drawn.shape.index(max(drawn.shape))
    beside = place[:main_axis] + [(place[main_axis] + 1) % drawn.shape[main_axis]] + place[main_axis + 1:]
    return drawn.at[tuple(place)].set(smallest).at[tuple(beside)].set(largest)


def block_scale(key, dims, pieces, low, high):
    def one(axis_at, shards_of):
        heights = jax.random.uniform(jax.random.fold_in(jax.random.fold_in(key, 6), axis_at), (shards_of,), jnp.float32, low / len(pieces), high / len(pieces))
        return jnp.repeat(jnp.exp(heights), dims[axis_at] // shards_of).reshape((-1,) + (1,) * (len(dims) - axis_at - 1))

    factor_of = one(*pieces[0])
    for cut in pieces[1:]:
        factor_of = factor_of * one(*cut)
    return factor_of


def normal_values(own_key, shape, deviation, reach, pieces=(), dtype=jnp.bfloat16):
    loudness = block_scale(own_key, shape, pieces, -0.22, 0.18) if pieces else 1.0
    values = jax.random.normal(own_key, shape, jnp.float32) * deviation * loudness
    return jnp.minimum(jnp.maximum(values, -reach), reach).astype(dtype)


def setup_inputs(seed: int = 0) -> dict:
    streams_of = jax.random.split(jax.random.key(seed), 6)
    return {
        "adjacency": normal_values(streams_of[0], (ROWS, COLS), (COLS // 2) ** -0.5, 0.0625, ((0, 64), (1, 16))),
        "block_mask": with_ends((jax.random.randint(streams_of[1], (ROWS // TILE, COLS // TILE), 0, 2) < 1).astype(jnp.int32), jax.random.fold_in(streams_of[1], 1), 0, 1),
        "features": normal_values(streams_of[2], (COLS, F), 1.0, 6.0, ((0, 1024),)),
        "weight": normal_values(streams_of[3], (F, F), F ** -0.5, 0.25),
        "upstream": draw_upstream(jax.random.fold_in(streams_of[5], 71), 0),
    }


def expand_mask(mask_tiles):
    return jnp.repeat(jnp.repeat(mask_tiles, TILE, 0), TILE, 1).astype(jnp.bfloat16)


def reference(adjacency, block_mask, features, weight, upstream):
    blocks = ROWS // PANEL_ROWS
    adj_blocks = adjacency.reshape(blocks, PANEL_ROWS, COLS)
    mask_blocks = block_mask.reshape(blocks, PANEL_ROWS // TILE, COLS // TILE)

    def forward_block(pair):
        masked = pair[0] * expand_mask(pair[1])
        return jnp.dot(masked, features, preferred_element_type=jnp.float32)

    aggregate = lax.map(forward_block, (adj_blocks, mask_blocks)).reshape(ROWS, F).astype(jnp.bfloat16)
    pre = jnp.dot(aggregate, weight, preferred_element_type=jnp.float32)
    output = jax.nn.silu(pre).astype(jnp.bfloat16)
    sigma = jax.nn.sigmoid(pre)
    dpre = (upstream.astype(jnp.float32) * sigma * (1.0 + pre * (1.0 - sigma))).astype(jnp.bfloat16)
    grad_in = jnp.dot(dpre, weight.T, preferred_element_type=jnp.float32).astype(jnp.bfloat16)
    grad_blocks = grad_in.reshape(blocks, PANEL_ROWS, F)

    def back_step(total, triple):
        masked = triple[0] * expand_mask(triple[1])
        return total + jnp.dot(masked.T, triple[2], preferred_element_type=jnp.float32), None

    feature_grad, unused = lax.scan(back_step, jnp.zeros((COLS, F), jnp.float32), (adj_blocks, mask_blocks, grad_blocks))
    weight_grad = jnp.dot(aggregate.T, dpre, preferred_element_type=jnp.float32) * (ROWS ** -0.5)
    return output, feature_grad, weight_grad
```

```python
import jax
import jax.numpy as jnp
from jax import lax
from jax.sharding import Mesh, PartitionSpec as P

TILE = 256
F32 = jnp.float32
BF16 = jnp.bfloat16


def exchange(chunks, axis):
    return lax.all_to_all(chunks, axis, split_axis=0, concat_axis=0, tiled=True)


def gather(block, axis):
    n = lax.axis_size(axis)
    return exchange(jnp.broadcast_to(block[None], (n,) + block.shape), axis)


def shards(adjacency, block_mask, features, weight, upstream):
    rows, cols = adjacency.shape
    width = features.shape[1]
    nz, nyl, ncore, nx, nyh = (lax.axis_size(a) for a in ("z", "yl", "core", "x", "yh"))
    n_row, n_col = nz * nyl * ncore, nx * nyh
    masked = adjacency * jnp.repeat(jnp.repeat(block_mask, TILE, 0), TILE, 1).astype(BF16)

    own = features.shape[0]
    by_z = gather(features, "z")
    by_yl = gather(by_z, "yl")
    by_core = gather(by_yl, "core")
    panel = by_core.transpose(2, 1, 0, 3, 4).reshape(cols, width)

    partial = jnp.dot(masked, panel, preferred_element_type=F32).astype(BF16)
    over_x = exchange(partial.reshape(nx, rows // nx, width), "x")
    summed_x = over_x.astype(F32).sum(0).astype(BF16)
    over_yh = exchange(summed_x.reshape(nyh, rows // n_col, width), "yh")
    aggregate = over_yh.astype(F32).sum(0).astype(BF16)

    pre = jnp.dot(aggregate, weight, preferred_element_type=F32)
    sigma = jax.nn.sigmoid(pre)
    output = (pre * sigma).astype(BF16)
    dpre = (upstream.astype(F32) * sigma * (1.0 + pre * (1.0 - sigma))).astype(BF16)

    both = jnp.concatenate([aggregate, dpre], axis=1)
    both = gather(gather(both, "yh").reshape(rows // nx, 2 * width), "x").reshape(rows, 2 * width)
    agg_all, dpre_all = both[:, :width], both[:, width:]
    grad_in = lax.dot_general(
        dpre_all, weight, (((1,), (1,)), ((), ())), preferred_element_type=F32
    ).astype(BF16)
    partial_fg = lax.dot_general(masked, grad_in, (((0,), (0,)), ((), ())), preferred_element_type=F32)
    slab = width // nx
    agg_slab = lax.dynamic_slice_in_dim(agg_all, lax.axis_index("x") * slab, slab, axis=1)
    partial_w = lax.dot_general(agg_slab, dpre_all, (((0,), (0,)), ((), ())), preferred_element_type=F32)

    chunk = cols // n_row
    fg = partial_fg.astype(BF16).reshape(nz, nyl, ncore, chunk, width).transpose(2, 1, 0, 3, 4)
    w = partial_w.astype(BF16)

    def fold(fg, w, axis, n):
        feet = fg.reshape(n, -1, width)
        send = jnp.concatenate([feet, jnp.broadcast_to(w[None], (n,) + w.shape)], axis=1)
        got = exchange(send, axis).astype(F32).sum(0).astype(BF16)
        return got[: feet.shape[1]], got[feet.shape[1] :]

    fg, w = fold(fg, w, "core", ncore)
    fg, w = fold(fg, w, "yl", nyl)
    send = jnp.concatenate([fg.reshape(nz, chunk, width), w.reshape(nz, slab // nz, width)], axis=1)
    got = exchange(send, "z").astype(F32).sum(0)
    feature_grad = got[:chunk]
    w_own = (got[chunk:] * (rows * n_row) ** (-0.5)).astype(BF16)
    weight_grad = gather(gather(w_own, "z").reshape(slab, width), "x").reshape(width, width).astype(F32)
    return (output, feature_grad, weight_grad)


def solution(mesh):
    fine = Mesh(mesh.devices.reshape(16, 2, 2, 4, 4), ("z", "yl", "core", "x", "yh"))
    row, col = ("z", "yl", "core"), ("x", "yh")
    return jax.shard_map(
        shards,
        mesh=fine,
        in_specs=(P(row, col), P(row, col), P(col + row, None), P(), P(row + col, None)),
        out_specs=(P(row + col, None), P(col + row, None), P()),
        check_vma=False,
    )
```

```python
import jax
import jax.numpy as jnp
from jax import lax
from jax.sharding import Mesh, PartitionSpec as P

TILE = 256
F32 = jnp.float32
BF16 = jnp.bfloat16


def exchange(chunks, axis):
    return lax.all_to_all(chunks, axis, split_axis=0, concat_axis=0, tiled=True)


def gather(block, axis):
    n = lax.axis_size(axis)
    return exchange(jnp.broadcast_to(block[None], (n,) + block.shape), axis)


def shards(adjacency, block_mask, features, weight, upstream):
    rows, cols = adjacency.shape
    width = features.shape[1]
    nz, nyl, ncore, nx, nyh = (lax.axis_size(a) for a in ("z", "yl", "core", "x", "yh"))
    n_row, n_col = nz * nyl * ncore, nx * nyh
    masked = adjacency * jnp.repeat(jnp.repeat(block_mask, TILE, 0), TILE, 1).astype(BF16)

    n = lax.axis_index
    up_all = lax.all_gather(upstream.astype(F32), ("x", "yh"), axis=0, tiled=True)
    panel = gather(gather(gather(features, "z"), "yl"), "core")
    panel = panel.transpose(2, 1, 0, 3, 4).reshape(cols, width)

    partial = jnp.dot(masked, panel, preferred_element_type=F32).astype(BF16)
    over_x = exchange(partial.reshape(nx, rows // nx, width), "x")
    aggregate = gather(over_x.astype(F32).sum(0).astype(BF16), "yh").astype(F32).sum(0).astype(BF16)
    own = lax.dynamic_slice_in_dim(aggregate, n("yh") * (rows // n_col), rows // n_col, axis=0)
    pre = jnp.dot(own, weight, preferred_element_type=F32)
    output = (pre * jax.nn.sigmoid(pre)).astype(BF16)

    agg_all = gather(aggregate, "x").reshape(rows, width)
    pre = jnp.dot(agg_all, weight, preferred_element_type=F32)
    sigma = jax.nn.sigmoid(pre)
    dpre_all = (up_all * sigma * (1.0 + pre * (1.0 - sigma))).astype(BF16)
    grad_in = lax.dot_general(
        dpre_all, weight, (((1,), (1,)), ((), ())), preferred_element_type=F32
    ).astype(BF16)
    partial_fg = lax.dot_general(masked, grad_in, (((0,), (0,)), ((), ())), preferred_element_type=F32)
    slab = width // n_col
    agg_slab = lax.dynamic_slice_in_dim(agg_all, n(("yh", "x")) * slab, slab, axis=1)
    w = lax.dot_general(agg_slab, dpre_all, (((0,), (0,)), ((), ())), preferred_element_type=F32)

    chunk, piece = cols // n_row, slab // (ncore * nyl)
    fg = partial_fg.astype(BF16).reshape(nz, nyl, ncore, chunk, width).transpose(2, 1, 0, 3, 4)
    fg = fg.reshape(ncore, nyl * nz * chunk, width)
    w = w.astype(BF16).reshape(ncore, nyl * piece, width)
    both = exchange(jnp.concatenate([fg, w], axis=1), "core").astype(F32).sum(0).astype(BF16)
    fg = both[: nyl * nz * chunk].reshape(nyl, nz * chunk, width)
    w = both[nyl * nz * chunk :].reshape(nyl, piece, width)
    both = exchange(jnp.concatenate([fg, w], axis=1), "yl").astype(F32).sum(0).astype(BF16)
    fg = both[: nz * chunk].reshape(nz, chunk, width)
    w = jnp.broadcast_to(both[nz * chunk :][None], (nz, piece, width))
    both = exchange(jnp.concatenate([fg, w], axis=1), "z").astype(F32).sum(0)
    feature_grad = both[:chunk]
    w = (both[chunk:] * (rows * n_row) ** (-0.5)).astype(BF16)
    w = gather(w, ("yl", "yh"))
    w = gather(w, ("x", "core"))
    w = w.reshape(nx, ncore, nyl, nyh, piece, width).transpose(3, 0, 1, 2, 4, 5)
    weight_grad = w.astype(F32).reshape(width, width)
    return (output, feature_grad, weight_grad)


def solution(mesh):
    fine = Mesh(mesh.devices.reshape(16, 2, 2, 4, 4), ("z", "yl", "core", "x", "yh"))
    row, col = ("z", "yl", "core"), ("x", "yh")
    return jax.shard_map(
        shards,
        mesh=fine,
        in_specs=(P(row, col), P(row, col), P(col + row, None), P(), P(row + col, None)),
        out_specs=(P(row + col, None), P(col + row, None), P()),
        check_vma=False,
    )
```

```python
import jax
import jax.numpy as jnp
from jax import lax
from jax.sharding import Mesh, PartitionSpec as P

TILE = 256
F32 = jnp.float32
BF16 = jnp.bfloat16


def exchange(chunks, axis):
    return lax.all_to_all(chunks, axis, split_axis=0, concat_axis=0, tiled=True)


def gather(block, axis):
    n = lax.axis_size(axis)
    return exchange(jnp.broadcast_to(block[None], (n,) + block.shape), axis)


def shards(adjacency, block_mask, features, weight, upstream):
    rows, cols = adjacency.shape
    width = features.shape[1]
    nz, nyl, ncore, nx, nyh = (lax.axis_size(a) for a in ("z", "yl", "core", "x", "yh"))
    n_row, n_col = nz * nyl * ncore, nx * nyh
    masked = adjacency * jnp.repeat(jnp.repeat(block_mask, TILE, 0), TILE, 1).astype(BF16)

    n = lax.axis_index
    panel = gather(gather(gather(features, "z"), "yl"), "core")
    panel = panel.transpose(2, 1, 0, 3, 4).reshape(cols, width)

    partial = jnp.dot(masked, panel, preferred_element_type=F32).astype(BF16)
    over_col = exchange(partial.reshape(n_col, rows // n_col, width), ("x", "yh"))
    aggregate = over_col.astype(F32).sum(0).astype(BF16)
    pre = jnp.dot(aggregate, weight, preferred_element_type=F32)
    sigma = jax.nn.sigmoid(pre)
    output = (pre * sigma).astype(BF16)
    dpre = (upstream.astype(F32) * sigma * (1.0 + pre * (1.0 - sigma))).astype(BF16)

    both = gather(jnp.concatenate([aggregate, dpre], axis=1), "yh").reshape(rows // nx, 2 * width)
    slab = width // nyh
    agg_slab = lax.dynamic_slice_in_dim(both, n("yh") * slab, slab, axis=1)
    dpre_x = both[:, width:]
    w = lax.dot_general(agg_slab, dpre_x, (((0,), (0,)), ((), ())), preferred_element_type=F32)
    w = w.astype(BF16).reshape(nx, slab // nx, width)
    dpre_x = jnp.broadcast_to(dpre_x[None], (nx,) + dpre_x.shape)
    both = exchange(jnp.concatenate([dpre_x, w], axis=1), "x")
    dpre_all = both[:, : rows // nx].reshape(rows, width)
    w = both[:, rows // nx :].astype(F32).sum(0)
    slab = width // n_col
    grad_in = lax.dot_general(
        dpre_all, weight, (((1,), (1,)), ((), ())), preferred_element_type=F32
    ).astype(BF16)
    partial_fg = lax.dot_general(masked, grad_in, (((0,), (0,)), ((), ())), preferred_element_type=F32)

    chunk, piece = cols // n_row, slab // (ncore * nyl)
    fg = partial_fg.astype(BF16).reshape(nz, nyl, ncore, chunk, width).transpose(2, 1, 0, 3, 4)
    fg = fg.reshape(ncore, nyl * nz * chunk, width)
    w = w.astype(BF16).reshape(ncore, nyl * piece, width)
    both = exchange(jnp.concatenate([fg, w], axis=1), "core").astype(F32).sum(0).astype(BF16)
    fg = both[: nyl * nz * chunk].reshape(nyl, nz * chunk, width)
    w = both[nyl * nz * chunk :].reshape(nyl, piece, width)
    both = exchange(jnp.concatenate([fg, w], axis=1), "yl").astype(F32).sum(0).astype(BF16)
    fg = both[: nz * chunk].reshape(nz, chunk, width)
    w = jnp.broadcast_to(both[nz * chunk :][None], (nz, piece, width))
    both = exchange(jnp.concatenate([fg, w], axis=1), "z").astype(F32).sum(0)
    feature_grad = both[:chunk]
    w = (both[chunk:] * (rows * n_row) ** (-0.5)).astype(BF16)
    w = gather(w, ("yl", "yh"))
    w = gather(w, ("x", "core"))
    w = w.reshape(nx, ncore, nyl, nyh, piece, width).transpose(3, 0, 1, 2, 4, 5)
    weight_grad = w.astype(F32).reshape(width, width)
    return (output, feature_grad, weight_grad)


def solution(mesh):
    fine = Mesh(mesh.devices.reshape(16, 2, 2, 4, 4), ("z", "yl", "core", "x", "yh"))
    row, col = ("z", "yl", "core"), ("x", "yh")
    return jax.shard_map(
        shards,
        mesh=fine,
        in_specs=(P(row, col), P(row, col), P(col + row, None), P(), P(row + col, None)),
        out_specs=(P(row + col, None), P(col + row, None), P()),
        check_vma=False,
    )
```

```python
import jax
import jax.numpy as jnp
from jax import lax
from jax.sharding import Mesh, PartitionSpec as P

TILE = 256
F32 = jnp.float32
BF16 = jnp.bfloat16


def exchange(chunks, axis):
    return lax.all_to_all(chunks, axis, split_axis=0, concat_axis=0, tiled=True)


def gather(block, axis):
    n = lax.axis_size(axis)
    return exchange(jnp.broadcast_to(block[None], (n,) + block.shape), axis)


def halve(pair, axis):
    me = lax.axis_index(axis)
    theirs = lax.dynamic_index_in_dim(pair, 1 - me, 0, keepdims=False)
    mine = lax.dynamic_index_in_dim(pair, me, 0, keepdims=False)
    got = lax.ppermute(theirs, axis, [(0, 1), (1, 0)])
    return (mine.astype(F32) + got.astype(F32)).astype(BF16)


def pass_round(block, axis):
    n, me = lax.axis_size(axis), lax.axis_index(axis)
    got = [block]
    for k in range(1, n):
        got.append(lax.ppermute(block, axis, [((i + k) % n, i) for i in range(n)]))
    both = jnp.stack(got + got[:-1])
    return lax.dynamic_slice_in_dim(both, (n - me) % n, n, axis=0)


def shards(adjacency, block_mask, features, weight, upstream):
    rows, cols = adjacency.shape
    width = features.shape[1]
    nz, nyl, ncore, nx, nyh = (lax.axis_size(a) for a in ("z", "yl", "core", "x", "yh"))
    n_row, n_col = nz * nyl * ncore, nx * nyh
    masked = adjacency * jnp.repeat(jnp.repeat(block_mask, TILE, 0), TILE, 1).astype(BF16)

    n = lax.axis_index
    panel = gather(gather(gather(features, "z"), "yl"), "core")
    panel = panel.transpose(2, 1, 0, 3, 4).reshape(cols, width)

    partial = jnp.dot(masked, panel, preferred_element_type=F32).astype(BF16)
    over_col = exchange(partial.reshape(n_col, rows // n_col, width), ("x", "yh"))
    aggregate = over_col.astype(F32).sum(0).astype(BF16)
    pre = jnp.dot(aggregate, weight, preferred_element_type=F32)
    sigma = jax.nn.sigmoid(pre)
    output = (pre * sigma).astype(BF16)
    dpre = (upstream.astype(F32) * sigma * (1.0 + pre * (1.0 - sigma))).astype(BF16)

    both = gather(jnp.concatenate([aggregate, dpre], axis=1), "yh").reshape(rows // nx, 2 * width)
    agg_x, dpre_x = both[:, :width], both[:, width:]
    w = lax.dot_general(agg_x, dpre_x, (((0,), (0,)), ((), ())), preferred_element_type=F32)
    slab = width // n_col
    w = lax.dynamic_index_in_dim(w.reshape(nx, nyh, slab, width), n("yh"), axis=1, keepdims=False)
    dpre_x = jnp.broadcast_to(dpre_x[None], (nx,) + dpre_x.shape)
    both = exchange(jnp.concatenate([dpre_x, w.astype(BF16)], axis=1), "x")
    dpre_all = both[:, : rows // nx].reshape(rows, width)
    w = both[:, rows // nx :].astype(F32).sum(0).astype(BF16)

    chunk, piece = cols // n_row, slab // (ncore * nyl)
    w = exchange(w.reshape(nyl * ncore, piece, width), ("yl", "core")).astype(F32).sum(0).astype(BF16)
    w = gather(w, "z").astype(F32).sum(0) * (rows * n_row) ** (-0.5)
    w = w.astype(BF16)

    grad_in = lax.dot_general(
        dpre_all, weight, (((1,), (1,)), ((), ())), preferred_element_type=F32
    ).astype(BF16)
    partial_fg = lax.dot_general(masked, grad_in, (((0,), (0,)), ((), ())), preferred_element_type=F32)
    fg = partial_fg.astype(BF16).reshape(nz, nyl, ncore, chunk, width).transpose(2, 1, 0, 3, 4)
    fg = halve(fg, "core")
    fg = halve(fg, "yl")
    fg, w = lax.optimization_barrier((fg, w))
    feature_grad = exchange(fg, "z").astype(F32).sum(0)

    w = pass_round(w, ("yl", "core"))
    w = pass_round(w.reshape(slab, width), "yh")
    w, feature_grad = lax.optimization_barrier((w, feature_grad))
    w = gather(w.reshape(slab * nyh, width), "x")
    return (output, feature_grad, w.astype(F32).reshape(width, width))


def solution(mesh):
    fine = Mesh(mesh.devices.reshape(16, 2, 2, 4, 4), ("z", "yl", "core", "x", "yh"))
    row, col = ("z", "yl", "core"), ("x", "yh")
    return jax.shard_map(
        shards,
        mesh=fine,
        in_specs=(P(row, col), P(row, col), P(col + row, None), P(), P(row + col, None)),
        out_specs=(P(row + col, None), P(col + row, None), P()),
        check_vma=False,
    )
```

```python
import jax
import jax.numpy as jnp
from jax import lax
from jax.sharding import Mesh, PartitionSpec as P

TILE = 256
F32 = jnp.float32
BF16 = jnp.bfloat16


def exchange(chunks, axis):
    return lax.all_to_all(chunks, axis, split_axis=0, concat_axis=0, tiled=True)


def gather(block, axis):
    n = lax.axis_size(axis)
    return exchange(jnp.broadcast_to(block[None], (n,) + block.shape), axis)


def halve(pair, axis):
    me = lax.axis_index(axis)
    theirs = lax.dynamic_index_in_dim(pair, 1 - me, 0, keepdims=False)
    mine = lax.dynamic_index_in_dim(pair, me, 0, keepdims=False)
    got = lax.ppermute(theirs, axis, [(0, 1), (1, 0)])
    return (mine.astype(F32) + got.astype(F32)).astype(BF16)


def shards(adjacency, block_mask, features, weight, upstream):
    rows, cols = adjacency.shape
    width = features.shape[1]
    nz, nyl, ncore, nx, nyh = (lax.axis_size(a) for a in ("z", "yl", "core", "x", "yh"))
    n_row, n_col = nz * nyl * ncore, nx * nyh
    masked = adjacency * jnp.repeat(jnp.repeat(block_mask, TILE, 0), TILE, 1).astype(BF16)

    n = lax.axis_index
    panel = gather(gather(gather(features, "z"), "yl"), "core")
    panel = panel.transpose(2, 1, 0, 3, 4).reshape(cols, width)

    partial = jnp.dot(masked, panel, preferred_element_type=F32).astype(BF16)
    over_col = exchange(partial.reshape(n_col, rows // n_col, width), ("x", "yh"))
    aggregate = over_col.astype(F32).sum(0).astype(BF16)
    pre = jnp.dot(aggregate, weight, preferred_element_type=F32)
    sigma = jax.nn.sigmoid(pre)
    output = (pre * sigma).astype(BF16)
    dpre = (upstream.astype(F32) * sigma * (1.0 + pre * (1.0 - sigma))).astype(BF16)

    both = gather(jnp.concatenate([aggregate, dpre], axis=1), "yh").reshape(rows // nx, 2 * width)
    agg_x, dpre_x = both[:, :width], both[:, width:]
    w = lax.dot_general(agg_x, dpre_x, (((0,), (0,)), ((), ())), preferred_element_type=F32)
    slab = width // n_col
    w = lax.dynamic_index_in_dim(w.reshape(nx, nyh, slab, width), n("yh"), axis=1, keepdims=False)
    dpre_x = jnp.broadcast_to(dpre_x[None], (nx,) + dpre_x.shape)
    both = exchange(jnp.concatenate([dpre_x, w.astype(BF16)], axis=1), "x")
    dpre_all = both[:, : rows // nx].reshape(rows, width)
    w = both[:, rows // nx :].astype(F32).sum(0).astype(BF16)

    chunk, piece = cols // n_row, slab // (ncore * nyl)
    w = exchange(w.reshape(nyl * ncore, piece, width), ("yl", "core")).astype(F32).sum(0).astype(BF16)
    w = gather(w, "z").astype(F32).sum(0) * (rows * n_row) ** (-0.5)
    w = w.astype(BF16)

    grad_in = lax.dot_general(
        dpre_all, weight, (((1,), (1,)), ((), ())), preferred_element_type=F32
    ).astype(BF16)
    partial_fg = lax.dot_general(masked, grad_in, (((0,), (0,)), ((), ())), preferred_element_type=F32)
    fg = partial_fg.astype(BF16).reshape(nz, nyl, ncore, chunk, width).transpose(2, 1, 0, 3, 4)
    fg = halve(fg, "core")
    fg = halve(fg, "yl")
    fg, w = lax.optimization_barrier((fg, w))
    feature_grad = exchange(fg, "z").astype(F32).sum(0)

    w = lax.all_gather(w, "core", axis=0, tiled=True)
    w = lax.all_gather(w, "yl", axis=0, tiled=True)
    w = lax.all_gather(w, "yh", axis=0, tiled=True)
    w, feature_grad = lax.optimization_barrier((w, feature_grad))
    w = gather(w, "x")
    return (output, feature_grad, w.astype(F32).reshape(width, width))


def solution(mesh):
    fine = Mesh(mesh.devices.reshape(16, 2, 2, 4, 4), ("z", "yl", "core", "x", "yh"))
    row, col = ("z", "yl", "core"), ("x", "yh")
    return jax.shard_map(
        shards,
        mesh=fine,
        in_specs=(P(row, col), P(row, col), P(col + row, None), P(), P(row + col, None)),
        out_specs=(P(row + col, None), P(col + row, None), P()),
        check_vma=False,
    )
```

```python
import jax
import jax.numpy as jnp
from jax import lax
from jax.sharding import Mesh, PartitionSpec as P

TILE = 256
F32 = jnp.float32
BF16 = jnp.bfloat16


def exchange(chunks, axis):
    return lax.all_to_all(chunks, axis, split_axis=0, concat_axis=0, tiled=True)


def gather(block, axis):
    n = lax.axis_size(axis)
    return exchange(jnp.broadcast_to(block[None], (n,) + block.shape), axis)


def halve(pair, axis, at):
    theirs = lax.dynamic_index_in_dim(pair, at["other_" + axis], 0, keepdims=False)
    mine = lax.dynamic_index_in_dim(pair, at[axis], 0, keepdims=False)
    got = lax.ppermute(theirs, axis, [(0, 1), (1, 0)])
    return (mine.astype(F32) + got.astype(F32)).astype(BF16)


def shards(adjacency, block_mask, features, weight, upstream):
    rows, cols = adjacency.shape
    width = features.shape[1]
    nz, nyl, ncore, nx, nyh = (lax.axis_size(a) for a in ("z", "yl", "core", "x", "yh"))
    n_row, n_col = nz * nyl * ncore, nx * nyh
    own = rows // n_col
    at = {a: lax.axis_index(a).astype(jnp.uint32) for a in ("yl", "core", "yh")}
    at.update(other_yl=1 - at["yl"], other_core=1 - at["core"], own_row=at["yh"] * own)
    features, at = lax.optimization_barrier((features, at))

    by_z = gather(features, "z")
    masked = adjacency * jnp.repeat(jnp.repeat(block_mask, TILE, 0), TILE, 1).astype(BF16)
    upstream_x = lax.all_gather(upstream, "yh", axis=0, tiled=True)
    by_z, masked, upstream_x = lax.optimization_barrier((by_z, masked, upstream_x))
    panel = gather(gather(by_z, "yl"), "core")
    panel = panel.transpose(2, 1, 0, 3, 4).reshape(cols, width)

    partial = jnp.dot(masked, panel, preferred_element_type=F32).astype(BF16)
    over_x = exchange(partial.reshape(nx, rows // nx, width), "x")
    agg_x = gather(over_x.astype(F32).sum(0).astype(BF16), "yh").astype(F32).sum(0).astype(BF16)
    pre = jnp.dot(agg_x, weight, preferred_element_type=F32)
    sigma = jax.nn.sigmoid(pre)
    output_x = (pre * sigma).astype(BF16)
    dpre_x = (upstream_x.astype(F32) * sigma * (1.0 + pre * (1.0 - sigma))).astype(BF16)

    w = lax.dot_general(agg_x, dpre_x, (((0,), (0,)), ((), ())), preferred_element_type=F32)
    slab = width // n_col
    w = w.reshape(nx, nyl, nyh, slab // nyl, width)
    w = lax.dynamic_index_in_dim(w, at["yh"], axis=2, keepdims=False).reshape(nx, slab, width)
    dpre_x = jnp.broadcast_to(dpre_x[None], (nx,) + dpre_x.shape)
    both = exchange(jnp.concatenate([dpre_x, w.astype(BF16)], axis=1), "x")
    dpre_all = both[:, : rows // nx].reshape(rows, width)
    w = both[:, rows // nx :].astype(F32).sum(0).astype(BF16)

    chunk, piece = cols // n_row, slab // (ncore * nyl)
    w = exchange(w.reshape(nyl * ncore, piece, width), ("yl", "core")).astype(F32).sum(0).astype(BF16)
    w, output_x = lax.optimization_barrier((w, output_x))
    output = lax.dynamic_slice_in_dim(output_x, at["own_row"], own, axis=0)
    w = gather(w, "z").astype(F32).sum(0) * (rows * n_row) ** (-0.5)
    w = w.astype(BF16)

    grad_in = lax.dot_general(
        dpre_all, weight, (((1,), (1,)), ((), ())), preferred_element_type=F32
    ).astype(BF16)
    partial_fg = lax.dot_general(masked, grad_in, (((0,), (0,)), ((), ())), preferred_element_type=F32)
    fg = partial_fg.astype(BF16).reshape(nz, nyl, ncore, chunk, width).transpose(2, 1, 0, 3, 4)
    fg = halve(fg, "core", at)
    fg = halve(fg, "yl", at)
    fg, w, output = lax.optimization_barrier((fg, w, output))
    feature_grad = exchange(fg, "z").astype(F32).sum(0)

    w = lax.all_gather(w, "core", axis=0, tiled=True)
    w = lax.all_gather(w, ("yl", "yh"), axis=0, tiled=True)
    w, feature_grad = lax.optimization_barrier((w, feature_grad))
    w = gather(w, "x")
    return (output, feature_grad, w.astype(F32).reshape(width, width))


def solution(mesh):
    fine = Mesh(mesh.devices.reshape(16, 2, 2, 4, 4), ("z", "yl", "core", "x", "yh"))
    row, col = ("z", "yl", "core"), ("x", "yh")
    return jax.shard_map(
        shards,
        mesh=fine,
        in_specs=(P(row, col), P(row, col), P(col + row, None), P(), P(row + col, None)),
        out_specs=(P(row + col, None), P(col + row, None), P()),
        check_vma=False,
    )
```

```python
import jax
import jax.numpy as jnp
from jax import lax
from jax.sharding import Mesh, PartitionSpec as P

TILE = 256
F32 = jnp.float32
BF16 = jnp.bfloat16


def exchange(chunks, axis):
    return lax.all_to_all(chunks, axis, split_axis=0, concat_axis=0, tiled=True)


def gather(block, axis):
    n = lax.axis_size(axis)
    return exchange(jnp.broadcast_to(block[None], (n,) + block.shape), axis)


def shards(adjacency, block_mask, features, weight, upstream):
    rows, cols = adjacency.shape
    width = features.shape[1]
    nz, nyl, ncore, nx, nyh = (lax.axis_size(a) for a in ("z", "yl", "core", "x", "yh"))
    n_row, n_col = nz * nyl * ncore, nx * nyh
    own = rows // n_col
    at = {a: lax.axis_index(a).astype(jnp.uint32) for a in ("yh",)}
    at.update(own_row=at["yh"] * own)
    features, at = lax.optimization_barrier((features, at))

    by_z = gather(features, "z")
    masked = adjacency * jnp.repeat(jnp.repeat(block_mask, TILE, 0), TILE, 1).astype(BF16)
    upstream_x = lax.all_gather(upstream, "yh", axis=0, tiled=True)
    by_z, masked, upstream_x = lax.optimization_barrier((by_z, masked, upstream_x))
    panel = gather(gather(by_z, "yl"), "core")
    panel = panel.transpose(2, 1, 0, 3, 4).reshape(cols, width)

    partial = jnp.dot(masked, panel, preferred_element_type=F32).astype(BF16)
    over_x = exchange(partial.reshape(nx, rows // nx, width), "x")
    agg_x = gather(over_x.astype(F32).sum(0).astype(BF16), "yh").astype(F32).sum(0).astype(BF16)
    pre = jnp.dot(agg_x, weight, preferred_element_type=F32)
    sigma = jax.nn.sigmoid(pre)
    output_x = (pre * sigma).astype(BF16)
    dpre_x = (upstream_x.astype(F32) * sigma * (1.0 + pre * (1.0 - sigma))).astype(BF16)

    w = lax.dot_general(agg_x, dpre_x, (((0,), (0,)), ((), ())), preferred_element_type=F32)
    slab = width // n_col
    chunk, piece = cols // n_row, slab // (ncore * nyl)
    w = w.astype(BF16).reshape(nx, nyl * ncore, nyh, piece, width)
    w = lax.dynamic_index_in_dim(w, at["yh"], axis=2, keepdims=False).reshape(nx, slab, width)
    output = lax.dynamic_slice_in_dim(output_x, at["own_row"], own, axis=0)
    w, dpre_x, output = lax.optimization_barrier((w, dpre_x, output))
    dpre_x = jnp.broadcast_to(dpre_x[None], (nx,) + dpre_x.shape)
    both = exchange(jnp.concatenate([dpre_x, w], axis=1), "x")
    dpre_all = both[:, : rows // nx].reshape(rows, width)
    w = both[:, rows // nx :].astype(F32).sum(0).astype(BF16)

    grad_in = lax.dot_general(
        dpre_all, weight, (((1,), (1,)), ((), ())), preferred_element_type=F32
    ).astype(BF16)
    partial_fg = lax.dot_general(masked, grad_in, (((0,), (0,)), ((), ())), preferred_element_type=F32)
    fg = partial_fg.astype(BF16).reshape(nz, nyl, ncore, chunk, width).transpose(2, 1, 0, 3, 4)
    fg = fg.reshape(ncore, nyl * nz * chunk, width)
    w = w.reshape(nyl, ncore, piece, width).transpose(1, 0, 2, 3).reshape(ncore, nyl * piece, width)
    both = exchange(jnp.concatenate([fg, w], axis=1), "core").astype(F32).sum(0).astype(BF16)
    fg = both[: nyl * nz * chunk].reshape(nyl, nz * chunk, width)
    w = both[nyl * nz * chunk :].reshape(nyl, piece, width)
    both = exchange(jnp.concatenate([fg, w], axis=1), "yl").astype(F32).sum(0).astype(BF16)
    fg = both[: nz * chunk].reshape(nz, chunk, width)
    w = jnp.broadcast_to(both[nz * chunk :][None], (nz, piece, width))
    both = exchange(jnp.concatenate([fg, w], axis=1), "z").astype(F32).sum(0)
    w = (both[chunk:] * (rows * n_row) ** (-0.5)).astype(BF16)
    feature_grad, w = lax.optimization_barrier((both[:chunk], w))

    w = gather(w, ("yl", "core", "yh")).reshape(slab * nyh, width)
    w = gather(w, "x").reshape(width, width)
    return (output, feature_grad, w.astype(F32))


def solution(mesh):
    fine = Mesh(mesh.devices.reshape(16, 2, 2, 4, 4), ("z", "yl", "core", "x", "yh"))
    row, col = ("z", "yl", "core"), ("x", "yh")
    return jax.shard_map(
        shards,
        mesh=fine,
        in_specs=(P(row, col), P(row, col), P(col + row, None), P(), P(row + col, None)),
        out_specs=(P(row + col, None), P(col + row, None), P()),
        check_vma=False,
    )
```

```python
import jax
import jax.numpy as jnp
from jax import lax
from jax.sharding import Mesh, PartitionSpec as P

TILE = 256
F32 = jnp.float32
BF16 = jnp.bfloat16


def exchange(chunks, axis):
    return lax.all_to_all(chunks, axis, split_axis=0, concat_axis=0, tiled=True)


def gather(block, axis):
    n = lax.axis_size(axis)
    return exchange(jnp.broadcast_to(block[None], (n,) + block.shape), axis)


def halve(pair, axis, at):
    theirs = lax.dynamic_index_in_dim(pair, at["other_" + axis], 0, keepdims=False)
    mine = lax.dynamic_index_in_dim(pair, at[axis], 0, keepdims=False)
    got = lax.ppermute(theirs, axis, [(0, 1), (1, 0)])
    return (mine.astype(F32) + got.astype(F32)).astype(BF16)


def shards(adjacency, block_mask, features, weight, upstream):
    rows, cols = adjacency.shape
    width = features.shape[1]
    nz, nyl, ncore, nx, nyh = (lax.axis_size(a) for a in ("z", "yl", "core", "x", "yh"))
    n_row, n_col = nz * nyl * ncore, nx * nyh
    own = rows // n_col
    at = {a: lax.axis_index(a).astype(jnp.uint32) for a in ("yl", "core", "yh")}
    at.update(other_yl=1 - at["yl"], other_core=1 - at["core"], own_row=at["yh"] * own)
    features, at = lax.optimization_barrier((features, at))

    by_z = gather(features, "z")
    masked = adjacency * jnp.repeat(jnp.repeat(block_mask, TILE, 0), TILE, 1).astype(BF16)
    upstream_x = lax.all_gather(upstream, "yh", axis=0, tiled=True)
    by_z, masked, upstream_x = lax.optimization_barrier((by_z, masked, upstream_x))
    panel = gather(gather(by_z, "yl"), "core")
    panel = panel.transpose(2, 1, 0, 3, 4).reshape(cols, width)

    partial = jnp.dot(masked, panel, preferred_element_type=F32).astype(BF16)
    over_x = exchange(partial.reshape(nx, rows // nx, width), "x")
    over_yh = lax.all_gather(over_x.astype(F32).sum(0).astype(BF16), "yh")
    agg_x = over_yh.astype(F32).sum(0).astype(BF16)
    pre = jnp.dot(agg_x, weight, preferred_element_type=F32)
    sigma = jax.nn.sigmoid(pre)
    output_x = (pre * sigma).astype(BF16)
    dpre_x = (upstream_x.astype(F32) * sigma * (1.0 + pre * (1.0 - sigma))).astype(BF16)

    w = lax.dot_general(agg_x, dpre_x, (((0,), (0,)), ((), ())), preferred_element_type=F32)
    slab = width // n_col
    piece = slab // (ncore * nyl)
    w = w.reshape(nx, ncore * nyl, nyh, piece, width)
    w = lax.dynamic_index_in_dim(w, at["yh"], axis=2, keepdims=False).reshape(nx, slab, width)
    dpre_x = jnp.broadcast_to(dpre_x[None], (nx,) + dpre_x.shape)
    both = exchange(jnp.concatenate([dpre_x, w.astype(BF16)], axis=1), "x")
    dpre_all = both[:, : rows // nx].reshape(rows, width)
    w = both[:, rows // nx :].astype(F32).sum(0).astype(BF16)

    chunk = cols // n_row
    w = w.reshape(ncore, nyl, piece, width).transpose(1, 0, 2, 3).reshape(nyl * ncore, piece, width)
    w = exchange(w, ("yl", "core")).astype(F32).sum(0).astype(BF16)
    w, output_x = lax.optimization_barrier((w, output_x))
    output = lax.dynamic_slice_in_dim(output_x, at["own_row"], own, axis=0)
    w = gather(w, "z").astype(F32).sum(0) * (rows * n_row) ** (-0.5)
    w = w.astype(BF16)

    grad_in = lax.dot_general(
        dpre_all, weight, (((1,), (1,)), ((), ())), preferred_element_type=F32
    ).astype(BF16)
    partial_fg = lax.dot_general(masked, grad_in, (((0,), (0,)), ((), ())), preferred_element_type=F32)
    fg = partial_fg.astype(BF16).reshape(nz, nyl, ncore, chunk, width).transpose(2, 1, 0, 3, 4)
    fg = halve(fg, "core", at)
    fg = halve(fg, "yl", at)
    fg, w, output = lax.optimization_barrier((fg, w, output))
    feature_grad = exchange(fg, "z").astype(F32).sum(0)

    for axis in ("yh", "yl", "core"):
        w = lax.all_gather(w, axis, axis=0, tiled=True)
    w, feature_grad = lax.optimization_barrier((w, feature_grad))
    w = gather(w, "x")
    return (output, feature_grad, w.astype(F32).reshape(width, width))


def solution(mesh):
    fine = Mesh(mesh.devices.reshape(16, 2, 2, 4, 4), ("z", "yl", "core", "x", "yh"))
    row, col = ("z", "yl", "core"), ("x", "yh")
    return jax.shard_map(
        shards,
        mesh=fine,
        in_specs=(P(row, col), P(row, col), P(col + row, None), P(), P(row + col, None)),
        out_specs=(P(row + col, None), P(col + row, None), P()),
        check_vma=False,
    )
```

```python
import jax
import jax.numpy as jnp
from jax import lax
from jax.sharding import Mesh, PartitionSpec as P

TILE = 256
F32 = jnp.float32
BF16 = jnp.bfloat16


def exchange(chunks, axis):
    return lax.all_to_all(chunks, axis, split_axis=0, concat_axis=0, tiled=True)


def gather(block, axis):
    n = lax.axis_size(axis)
    return exchange(jnp.broadcast_to(block[None], (n,) + block.shape), axis)


def halve(pair, axis, at):
    theirs = lax.dynamic_index_in_dim(pair, at["other_" + axis], 0, keepdims=False)
    mine = lax.dynamic_index_in_dim(pair, at[axis], 0, keepdims=False)
    got = lax.ppermute(theirs, axis, [(0, 1), (1, 0)])
    return (mine.astype(F32) + got.astype(F32)).astype(BF16)


def shards(adjacency, block_mask, features, weight, upstream):
    rows, cols = adjacency.shape
    width = features.shape[1]
    nz, nyl, ncore, nx, nyh = (lax.axis_size(a) for a in ("z", "yl", "core", "x", "yh"))
    n_row, n_col = nz * nyl * ncore, nx * nyh
    own = rows // n_col
    at = {a: lax.axis_index(a).astype(jnp.uint32) for a in ("yl", "core", "yh")}
    at.update(other_yl=1 - at["yl"], other_core=1 - at["core"], own_row=at["yh"] * own)
    features, at = lax.optimization_barrier((features, at))

    by_z = gather(features, "z")
    masked = adjacency * jnp.repeat(jnp.repeat(block_mask, TILE, 0), TILE, 1).astype(BF16)
    upstream_x = lax.all_gather(upstream, "yh", axis=0, tiled=True)
    by_z, masked, upstream_x = lax.optimization_barrier((by_z, masked, upstream_x))
    panel = gather(gather(by_z, "yl"), "core")
    panel = panel.transpose(2, 1, 0, 3, 4).reshape(cols, width)

    partial = jnp.dot(masked, panel, preferred_element_type=F32).astype(BF16)
    over_x = exchange(partial.reshape(nx, rows // nx, width), "x")
    over_yh = lax.all_gather(over_x.astype(F32).sum(0).astype(BF16), "yh")
    agg_x = over_yh.astype(F32).sum(0).astype(BF16)
    pre = jnp.dot(agg_x, weight, preferred_element_type=F32)
    sigma = jax.nn.sigmoid(pre)
    output_x = (pre * sigma).astype(BF16)
    dpre_x = (upstream_x.astype(F32) * sigma * (1.0 + pre * (1.0 - sigma))).astype(BF16)

    w = lax.dot_general(agg_x, dpre_x, (((0,), (0,)), ((), ())), preferred_element_type=F32)
    slab = width // n_col
    piece = slab // (ncore * nyl)
    w = w.reshape(ncore, nx, nyl, nyh, piece, width)
    w = lax.dynamic_index_in_dim(w, at["yh"], axis=3, keepdims=False)
    w = w.transpose(2, 0, 1, 3, 4).reshape(nyl * ncore * nx, piece, width).astype(BF16)
    w = exchange(w, ("yl", "core", "x")).astype(F32).sum(0).astype(BF16)
    dpre_all = lax.all_gather(dpre_x, "x", axis=0, tiled=True)
    chunk = cols // n_row
    w, dpre_all, output_x = lax.optimization_barrier((w, dpre_all, output_x))
    output = lax.dynamic_slice_in_dim(output_x, at["own_row"], own, axis=0)
    w = gather(w, "z").astype(F32).sum(0) * (rows * n_row) ** (-0.5)
    w = w.astype(BF16)

    grad_in = lax.dot_general(
        dpre_all, weight, (((1,), (1,)), ((), ())), preferred_element_type=F32
    ).astype(BF16)
    partial_fg = lax.dot_general(masked, grad_in, (((0,), (0,)), ((), ())), preferred_element_type=F32)
    fg = partial_fg.astype(BF16).reshape(nz, nyl, ncore, chunk, width).transpose(2, 1, 0, 3, 4)
    fg = halve(fg, "core", at)
    fg = halve(fg, "yl", at)
    fg, w, output = lax.optimization_barrier((fg, w, output))
    feature_grad = exchange(fg, "z").astype(F32).sum(0)

    for axis in ("yh", "yl"):
        w = lax.all_gather(w, axis, axis=0, tiled=True)
    w, feature_grad = lax.optimization_barrier((w, feature_grad))
    w = lax.all_gather(gather(w, "x").reshape(width // ncore, width), "core", axis=0, tiled=True)
    return (output, feature_grad, w.astype(F32).reshape(width, width))


def solution(mesh):
    fine = Mesh(mesh.devices.reshape(16, 2, 2, 4, 4), ("z", "yl", "core", "x", "yh"))
    row, col = ("z", "yl", "core"), ("x", "yh")
    return jax.shard_map(
        shards,
        mesh=fine,
        in_specs=(P(row, col), P(row, col), P(col + row, None), P(), P(row + col, None)),
        out_specs=(P(row + col, None), P(col + row, None), P()),
        check_vma=False,
    )
```

```python
import jax
import jax.numpy as jnp
from jax import lax
from jax.sharding import Mesh, PartitionSpec as P

TILE = 256
F32 = jnp.float32
BF16 = jnp.bfloat16


def exchange(chunks, axis):
    return lax.all_to_all(chunks, axis, split_axis=0, concat_axis=0, tiled=True)


def gather(block, axis):
    n = lax.axis_size(axis)
    return exchange(jnp.broadcast_to(block[None], (n,) + block.shape), axis)


def halve(pair, axis, at):
    theirs = lax.dynamic_index_in_dim(pair, at["other_" + axis], 0, keepdims=False)
    mine = lax.dynamic_index_in_dim(pair, at[axis], 0, keepdims=False)
    got = lax.ppermute(theirs, axis, [(0, 1), (1, 0)])
    return (mine.astype(F32) + got.astype(F32)).astype(BF16)


def shards(adjacency, block_mask, features, weight, upstream):
    rows, cols = adjacency.shape
    width = features.shape[1]
    nz, nyl, ncore, nx, nyh = (lax.axis_size(a) for a in ("z", "yl", "core", "x", "yh"))
    n_row, n_col = nz * nyl * ncore, nx * nyh
    own = rows // n_col
    at = {a: lax.axis_index(a).astype(jnp.uint32) for a in ("yl", "core", "yh")}
    at.update(other_yl=1 - at["yl"], other_core=1 - at["core"], own_row=at["yh"] * own)
    features, at = lax.optimization_barrier((features, at))

    by_z = gather(features, "z")
    masked = adjacency * jnp.repeat(jnp.repeat(block_mask, TILE, 0), TILE, 1).astype(BF16)
    upstream_x = lax.all_gather(upstream, "yh", axis=0, tiled=True)
    by_z, masked, upstream_x = lax.optimization_barrier((by_z, masked, upstream_x))
    panel = gather(gather(by_z, "yl"), "core")
    panel = panel.transpose(2, 1, 0, 3, 4).reshape(cols, width)

    partial = jnp.dot(masked, panel, preferred_element_type=F32).astype(BF16)
    over_x = exchange(partial.reshape(nx, rows // nx, width), "x")
    over_yh = lax.all_gather(over_x.astype(F32).sum(0).astype(BF16), "yh")
    agg_x = over_yh.astype(F32).sum(0).astype(BF16)
    pre = jnp.dot(agg_x, weight, preferred_element_type=F32)
    sigma = jax.nn.sigmoid(pre)
    output_x = (pre * sigma).astype(BF16)
    dpre_x = (upstream_x.astype(F32) * sigma * (1.0 + pre * (1.0 - sigma))).astype(BF16)

    w = lax.dot_general(agg_x, dpre_x, (((0,), (0,)), ((), ())), preferred_element_type=F32)
    slab = width // n_col
    piece = slab // (ncore * nyl)
    w = w.reshape(ncore, nx, nyl, nyh, piece, width)
    w = lax.dynamic_index_in_dim(w, at["yh"], axis=3, keepdims=False)
    w = w.transpose(2, 0, 1, 3, 4).reshape(nyl * ncore * nx, piece, width).astype(BF16)
    w = exchange(w, ("yl", "core", "x")).astype(F32).sum(0).astype(BF16)
    dpre_all = lax.all_gather(dpre_x, "x", axis=0, tiled=True)
    chunk = cols // n_row
    w = gather(w, "z").astype(F32).sum(0) * (rows * n_row) ** (-0.5)
    w = w.astype(BF16)

    grad_in = lax.dot_general(
        dpre_all, weight, (((1,), (1,)), ((), ())), preferred_element_type=F32
    ).astype(BF16)
    partial_fg = lax.dot_general(masked, grad_in, (((0,), (0,)), ((), ())), preferred_element_type=F32)
    fg = partial_fg.astype(BF16).reshape(nz, nyl, ncore, chunk, width).transpose(2, 1, 0, 3, 4)
    fg = halve(fg, "core", at)
    fg, output_x = lax.optimization_barrier((fg, output_x))
    output = lax.dynamic_slice_in_dim(output_x, at["own_row"], own, axis=0)
    fg = halve(fg, "yl", at)
    fg, w, output = lax.optimization_barrier((fg, w, output))
    feature_grad = exchange(fg, "z").astype(F32).sum(0)

    for axis in ("yh", "yl"):
        w = lax.all_gather(w, axis, axis=0, tiled=True)
    w, feature_grad = lax.optimization_barrier((w, feature_grad))
    w = lax.all_gather(gather(w, "x").reshape(width // ncore, width), "core", axis=0, tiled=True)
    return (output, feature_grad, w.astype(F32).reshape(width, width))


def solution(mesh):
    fine = Mesh(mesh.devices.reshape(16, 2, 2, 4, 4), ("z", "yl", "core", "x", "yh"))
    row, col = ("z", "yl", "core"), ("x", "yh")
    return jax.shard_map(
        shards,
        mesh=fine,
        in_specs=(P(row, col), P(row, col), P(col + row, None), P(), P(row + col, None)),
        out_specs=(P(row + col, None), P(col + row, None), P()),
        check_vma=False,
    )
```

```python
import jax
import jax.numpy as jnp
from jax import lax
from jax.sharding import Mesh, PartitionSpec as P

TILE = 256
F32 = jnp.float32
BF16 = jnp.bfloat16


def exchange(chunks, axis):
    return lax.all_to_all(chunks, axis, split_axis=0, concat_axis=0, tiled=True)


def gather(block, axis):
    n = lax.axis_size(axis)
    return exchange(jnp.broadcast_to(block[None], (n,) + block.shape), axis)


def halve(pair, axis, at):
    theirs = lax.dynamic_index_in_dim(pair, at["other_" + axis], 0, keepdims=False)
    mine = lax.dynamic_index_in_dim(pair, at[axis], 0, keepdims=False)
    got = lax.ppermute(theirs, axis, [(0, 1), (1, 0)])
    return (mine.astype(F32) + got.astype(F32)).astype(BF16)


def shards(adjacency, block_mask, features, weight, upstream):
    rows, cols = adjacency.shape
    width = features.shape[1]
    nz, nyl, ncore, nx, nyh = (lax.axis_size(a) for a in ("z", "yl", "core", "x", "yh"))
    n_row, n_col = nz * nyl * ncore, nx * nyh
    own = rows // n_col
    at = {a: lax.axis_index(a).astype(jnp.uint32) for a in ("yl", "core", "yh")}
    at.update(other_yl=1 - at["yl"], other_core=1 - at["core"], own_row=at["yh"] * own)
    features, at = lax.optimization_barrier((features, at))

    by_z = gather(features, "z")
    masked = adjacency * jnp.repeat(jnp.repeat(block_mask, TILE, 0), TILE, 1).astype(BF16)
    upstream_x = lax.all_gather(upstream, "yh", axis=0, tiled=True)
    by_z, masked, upstream_x = lax.optimization_barrier((by_z, masked, upstream_x))
    panel = gather(gather(by_z, "yl"), "core")
    panel = panel.transpose(2, 1, 0, 3, 4).reshape(cols, width)

    partial = jnp.dot(masked, panel, preferred_element_type=F32).astype(BF16)
    over_x = exchange(partial.reshape(nx, rows // nx, width), "x")
    over_yh = lax.all_gather(over_x.astype(F32).sum(0).astype(BF16), "yh")
    agg_x = over_yh.astype(F32).sum(0).astype(BF16)
    pre = jnp.dot(agg_x, weight, preferred_element_type=F32)
    sigma = jax.nn.sigmoid(pre)
    output_x = (pre * sigma).astype(BF16)
    dpre_x = (upstream_x.astype(F32) * sigma * (1.0 + pre * (1.0 - sigma))).astype(BF16)

    w = lax.dot_general(agg_x, dpre_x, (((0,), (0,)), ((), ())), preferred_element_type=F32)
    slab = width // n_col
    piece = slab // (ncore * nyl)
    w = w.reshape(ncore, nx, nyl, nyh, piece, width)
    w = lax.dynamic_index_in_dim(w, at["yh"], axis=3, keepdims=False)
    w = w.transpose(1, 2, 0, 3, 4).reshape(nx, slab, width)
    dpre_x = jnp.broadcast_to(dpre_x[None], (nx,) + dpre_x.shape)
    both = exchange(jnp.concatenate([dpre_x, w.astype(BF16)], axis=1), "x")
    dpre_all = jnp.concatenate([both[i, : rows // nx] for i in range(nx)], axis=0)
    w = both[:, rows // nx :].astype(F32).sum(0).astype(BF16)

    chunk = cols // n_row
    w = exchange(w.reshape(nyl * ncore, piece, width), ("yl", "core")).astype(F32).sum(0).astype(BF16)
    w, output_x = lax.optimization_barrier((w, output_x))
    output = lax.dynamic_slice_in_dim(output_x, at["own_row"], own, axis=0)
    w = gather(w, "z").astype(F32).sum(0) * (rows * n_row) ** (-0.5)
    w = w.astype(BF16)

    grad_in = lax.dot_general(
        dpre_all, weight, (((1,), (1,)), ((), ())), preferred_element_type=F32
    ).astype(BF16)
    partial_fg = lax.dot_general(masked, grad_in, (((0,), (0,)), ((), ())), preferred_element_type=F32)
    fg = partial_fg.astype(BF16).reshape(nz, nyl, ncore, chunk, width).transpose(2, 1, 0, 3, 4)
    fg = halve(fg, "core", at)
    fg = halve(fg, "yl", at)
    fg, w, output = lax.optimization_barrier((fg, w, output))
    feature_grad = exchange(fg, "z").astype(F32).sum(0)

    for axis in ("yh", "yl"):
        w = lax.all_gather(w, axis, axis=0, tiled=True)
    w, feature_grad = lax.optimization_barrier((w, feature_grad))
    w = lax.all_gather(gather(w, "x").reshape(width // ncore, width), "core", axis=0, tiled=True)
    return (output, feature_grad, w.astype(F32).reshape(width, width))


def solution(mesh):
    fine = Mesh(mesh.devices.reshape(16, 2, 2, 4, 4), ("z", "yl", "core", "x", "yh"))
    row, col = ("z", "yl", "core"), ("x", "yh")
    return jax.shard_map(
        shards,
        mesh=fine,
        in_specs=(P(row, col), P(row, col), P(col + row, None), P(), P(row + col, None)),
        out_specs=(P(row + col, None), P(col + row, None), P()),
        check_vma=False,
    )
```

```python
import jax
import jax.numpy as jnp
from jax import lax
from jax.experimental import pallas as pl
from jax.experimental.pallas import tpu as pltpu
from jax.sharding import Mesh, PartitionSpec as P

TILE = 256
F32 = jnp.float32
BF16 = jnp.bfloat16


def exchange(chunks, axis):
    return lax.all_to_all(chunks, axis, split_axis=0, concat_axis=0, tiled=True)


def gather(block, axis):
    n = lax.axis_size(axis)
    return exchange(jnp.broadcast_to(block[None], (n,) + block.shape), axis)


def halve(pair, axis, at):
    theirs = lax.dynamic_index_in_dim(pair, at["other_" + axis], 0, keepdims=False)
    mine = lax.dynamic_index_in_dim(pair, at[axis], 0, keepdims=False)
    got = lax.ppermute(theirs, axis, [(0, 1), (1, 0)])
    return (mine.astype(F32) + got.astype(F32)).astype(BF16)


def mask_rows(mask, adjacency, masked):
    i = pl.program_id(0)
    for j in range(adjacency.shape[1] // TILE):
        tile = pl.ds(j * TILE, TILE)
        scale = mask[i, j].astype(F32)
        masked[:, tile] = (adjacency[:, tile].astype(F32) * scale).astype(BF16)


def mask_tiles(adjacency, block_mask):
    rows, cols = adjacency.shape
    return pl.pallas_call(
        mask_rows,
        grid=(rows // TILE,),
        in_specs=[
            pl.BlockSpec(memory_space=pltpu.SMEM),
            pl.BlockSpec((TILE, cols), lambda i: (i, 0)),
        ],
        out_specs=pl.BlockSpec((TILE, cols), lambda i: (i, 0)),
        out_shape=jax.ShapeDtypeStruct((rows, cols), BF16),
        compiler_params=pltpu.CompilerParams(vmem_limit_bytes=60 * 2**20),
        cost_estimate=pl.CostEstimate(flops=rows * cols, bytes_accessed=4 * rows * cols, transcendentals=0),
    )(block_mask, adjacency)


def shards(adjacency, block_mask, features, weight, upstream):
    rows, cols = adjacency.shape
    width = features.shape[1]
    nz, nyl, ncore, nx, nyh = (lax.axis_size(a) for a in ("z", "yl", "core", "x", "yh"))
    n_row, n_col = nz * nyl * ncore, nx * nyh
    own = rows // n_col
    at = {a: lax.axis_index(a).astype(jnp.uint32) for a in ("yl", "core", "yh")}
    at.update(other_yl=1 - at["yl"], other_core=1 - at["core"], own_row=at["yh"] * own)
    features, at = lax.optimization_barrier((features, at))

    by_z = gather(features, "z")
    masked = mask_tiles(adjacency, block_mask)
    upstream_x = lax.all_gather(upstream, "yh", axis=0, tiled=True)
    by_z, masked, upstream_x = lax.optimization_barrier((by_z, masked, upstream_x))
    panel = gather(gather(by_z, "yl"), "core")
    panel = panel.transpose(2, 1, 0, 3, 4).reshape(cols, width)

    partial = jnp.dot(masked, panel, preferred_element_type=F32).astype(BF16)
    over_x = exchange(partial.reshape(nx, rows // nx, width), "x")
    over_yh = lax.all_gather(over_x.astype(F32).sum(0).astype(BF16), "yh")
    agg_x = over_yh.astype(F32).sum(0).astype(BF16)
    pre = jnp.dot(agg_x, weight, preferred_element_type=F32)
    sigma = jax.nn.sigmoid(pre)
    output_x = (pre * sigma).astype(BF16)
    dpre_x = (upstream_x.astype(F32) * sigma * (1.0 + pre * (1.0 - sigma))).astype(BF16)

    w = lax.dot_general(agg_x, dpre_x, (((0,), (0,)), ((), ())), preferred_element_type=F32)
    slab = width // n_col
    piece = slab // (ncore * nyl)
    w = w.reshape(ncore, nx, nyl, nyh, piece, width)
    w = lax.dynamic_index_in_dim(w, at["yh"], axis=3, keepdims=False)
    w = w.transpose(2, 0, 1, 3, 4).reshape(nyl * ncore * nx, piece, width).astype(BF16)
    w = exchange(w, ("yl", "core", "x")).astype(F32).sum(0).astype(BF16)
    dpre_all = lax.all_gather(dpre_x, "x", axis=0, tiled=True)
    chunk = cols // n_row
    w, dpre_all, output_x = lax.optimization_barrier((w, dpre_all, output_x))
    output = lax.dynamic_slice_in_dim(output_x, at["own_row"], own, axis=0)
    w = gather(w, "z").astype(F32).sum(0) * (rows * n_row) ** (-0.5)
    w = w.astype(BF16)

    grad_in = lax.dot_general(
        dpre_all, weight, (((1,), (1,)), ((), ())), preferred_element_type=F32
    ).astype(BF16)
    partial_fg = lax.dot_general(masked, grad_in, (((0,), (0,)), ((), ())), preferred_element_type=F32)
    fg = partial_fg.astype(BF16).reshape(nz, nyl, ncore, chunk, width).transpose(2, 1, 0, 3, 4)
    fg = halve(fg, "core", at)
    fg = halve(fg, "yl", at)
    fg, w, output = lax.optimization_barrier((fg, w, output))
    feature_grad = exchange(fg, "z").astype(F32).sum(0)

    for axis in ("yh", "yl"):
        w = lax.all_gather(w, axis, axis=0, tiled=True)
    w, feature_grad = lax.optimization_barrier((w, feature_grad))
    w = lax.all_gather(gather(w, "x").reshape(width // ncore, width), "core", axis=0, tiled=True)
    return (output, feature_grad, w.astype(F32).reshape(width, width))


def solution(mesh):
    fine = Mesh(mesh.devices.reshape(16, 2, 2, 4, 4), ("z", "yl", "core", "x", "yh"))
    row, col = ("z", "yl", "core"), ("x", "yh")
    return jax.shard_map(
        shards,
        mesh=fine,
        in_specs=(P(row, col), P(row, col), P(col + row, None), P(), P(row + col, None)),
        out_specs=(P(row + col, None), P(col + row, None), P()),
        check_vma=False,
    )
```

```python
import jax
import jax.numpy as jnp
from jax import lax
from jax.sharding import Mesh, PartitionSpec as P

TILE = 256
F32 = jnp.float32
BF16 = jnp.bfloat16


def exchange(chunks, axis):
    return lax.all_to_all(chunks, axis, split_axis=0, concat_axis=0, tiled=True)


def gather(block, axis):
    n = lax.axis_size(axis)
    return exchange(jnp.broadcast_to(block[None], (n,) + block.shape), axis)


def halve(pair, axis, at):
    theirs = lax.dynamic_index_in_dim(pair, at["other_" + axis], 0, keepdims=False)
    mine = lax.dynamic_index_in_dim(pair, at[axis], 0, keepdims=False)
    got = lax.ppermute(theirs, axis, [(0, 1), (1, 0)])
    return (mine.astype(F32) + got.astype(F32)).astype(BF16)


def shards(adjacency, block_mask, features, weight, upstream):
    rows, cols = adjacency.shape
    width = features.shape[1]
    nz, nyl, ncore, nx, nyh = (lax.axis_size(a) for a in ("z", "yl", "core", "x", "yh"))
    n_row, n_col = nz * nyl * ncore, nx * nyh
    own = rows // n_col
    at = {a: lax.axis_index(a).astype(jnp.uint32) for a in ("yl", "core", "yh")}
    at.update(other_yl=1 - at["yl"], other_core=1 - at["core"], own_row=at["yh"] * own)
    features, at = lax.optimization_barrier((features, at))

    by_z = gather(features, "z")
    masked = adjacency * jnp.repeat(jnp.repeat(block_mask, TILE, 0), TILE, 1).astype(BF16)
    upstream_x = lax.all_gather(upstream, "yh", axis=0, tiled=True)
    by_z, masked, upstream_x = lax.optimization_barrier((by_z, masked, upstream_x))
    panel = gather(gather(by_z, "yl"), "core")
    panel = panel.transpose(2, 1, 0, 3, 4).reshape(cols, width)

    partial = jnp.dot(masked, panel, preferred_element_type=F32).astype(BF16)
    over_x = exchange(partial.reshape(nx, rows // nx, width), "x")
    over_yh = lax.all_gather(over_x.astype(F32).sum(0).astype(BF16), "yh")
    agg_x = over_yh.astype(F32).sum(0).astype(BF16)
    pre = jnp.dot(agg_x, weight, preferred_element_type=F32)
    sigma = jax.nn.sigmoid(pre)
    output_x = (pre * sigma).astype(BF16)
    dpre_x = (upstream_x.astype(F32) * sigma * (1.0 + pre * (1.0 - sigma))).astype(BF16)

    w = lax.dot_general(agg_x, dpre_x, (((0,), (0,)), ((), ())), preferred_element_type=F32)
    slab = width // n_col
    piece = slab // (ncore * nyl)
    w = w.reshape(ncore, nx, nyl, nyh, piece, width)
    w = lax.dynamic_index_in_dim(w, at["yh"], axis=3, keepdims=False)
    w = w.transpose(1, 2, 0, 3, 4).reshape(nx, slab, width)
    dpre_x = jnp.broadcast_to(dpre_x[None], (nx,) + dpre_x.shape)
    both = exchange(jnp.concatenate([dpre_x, w.astype(BF16)], axis=1), "x")
    dpre_all = both[:, : rows // nx].reshape(rows, width)
    w = both[:, rows // nx :].astype(F32).sum(0).astype(BF16)

    chunk = cols // n_row
    w = exchange(w.reshape(nyl * ncore, piece, width), ("yl", "core")).astype(F32).sum(0).astype(BF16)
    w_sum, output_x = lax.optimization_barrier((w, output_x))
    output = lax.dynamic_slice_in_dim(output_x, at["own_row"], own, axis=0)

    grad_in = lax.dot_general(
        dpre_all, weight, (((1,), (1,)), ((), ())), preferred_element_type=F32
    ).astype(BF16)
    partial_fg = lax.dot_general(masked, grad_in, (((0,), (0,)), ((), ())), preferred_element_type=F32)
    fg = partial_fg.astype(BF16).reshape(nz, nyl, ncore, chunk, width).transpose(2, 1, 0, 3, 4)
    fg, w_sum = lax.optimization_barrier((fg, w_sum))
    w = gather(w_sum, "z").astype(F32).sum(0) * (rows * n_row) ** (-0.5)
    w = w.astype(BF16)
    fg = halve(fg, "core", at)
    fg = halve(fg, "yl", at)
    fg, w, output = lax.optimization_barrier((fg, w, output))
    feature_grad = exchange(fg, "z").astype(F32).sum(0)

    for axis in ("yh", "yl"):
        w = lax.all_gather(w, axis, axis=0, tiled=True)
    w, feature_grad = lax.optimization_barrier((w, feature_grad))
    w = lax.all_gather(gather(w, "x").reshape(width // ncore, width), "core", axis=0, tiled=True)
    return (output, feature_grad, w.astype(F32).reshape(width, width))


def solution(mesh):
    fine = Mesh(mesh.devices.reshape(16, 2, 2, 4, 4), ("z", "yl", "core", "x", "yh"))
    row, col = ("z", "yl", "core"), ("x", "yh")
    return jax.shard_map(
        shards,
        mesh=fine,
        in_specs=(P(row, col), P(row, col), P(col + row, None), P(), P(row + col, None)),
        out_specs=(P(row + col, None), P(col + row, None), P()),
        check_vma=False,
    )
```

```python
import jax
import jax.numpy as jnp
from jax import lax
from jax.sharding import Mesh, PartitionSpec as P

TILE = 256
F32 = jnp.float32
BF16 = jnp.bfloat16


def exchange(chunks, axis):
    return lax.all_to_all(chunks, axis, split_axis=0, concat_axis=0, tiled=True)


def gather(block, axis):
    n = lax.axis_size(axis)
    return exchange(jnp.broadcast_to(block[None], (n,) + block.shape), axis)


def halve(pair, axis, at):
    theirs = lax.dynamic_index_in_dim(pair, at["other_" + axis], 0, keepdims=False)
    mine = lax.dynamic_index_in_dim(pair, at[axis], 0, keepdims=False)
    got = lax.ppermute(theirs, axis, [(0, 1), (1, 0)])
    return (mine.astype(F32) + got.astype(F32)).astype(BF16)


def shards(adjacency, block_mask, features, weight, upstream):
    rows, cols = adjacency.shape
    width = features.shape[1]
    nz, nyl, ncore, nx, nyh = (lax.axis_size(a) for a in ("z", "yl", "core", "x", "yh"))
    n_row, n_col = nz * nyl * ncore, nx * nyh
    own = rows // n_col
    at = {a: lax.axis_index(a).astype(jnp.uint32) for a in ("yl", "core", "yh")}
    at.update(other_yl=1 - at["yl"], other_core=1 - at["core"], own_row=at["yh"] * own)
    features, at = lax.optimization_barrier((features, at))

    by_z = gather(features, "z")
    masked = adjacency * jnp.repeat(jnp.repeat(block_mask, TILE, 0), TILE, 1).astype(BF16)
    upstream_x = lax.all_gather(upstream, "yh", axis=0, tiled=True)
    by_z, upstream_x = lax.optimization_barrier((by_z, upstream_x))
    panel = gather(gather(by_z, "yl"), "core")
    panel = panel.transpose(2, 1, 0, 3, 4).reshape(cols, width)

    partial = jnp.dot(masked, panel, preferred_element_type=F32).astype(BF16)
    over_x = exchange(partial.reshape(nx, rows // nx, width), "x")
    over_yh = lax.all_gather(over_x.astype(F32).sum(0).astype(BF16), "yh")
    agg_x = over_yh.astype(F32).sum(0).astype(BF16)
    pre = jnp.dot(agg_x, weight, preferred_element_type=F32)
    sigma = jax.nn.sigmoid(pre)
    output_x = (pre * sigma).astype(BF16)
    dpre_x = (upstream_x.astype(F32) * sigma * (1.0 + pre * (1.0 - sigma))).astype(BF16)

    w = lax.dot_general(agg_x, dpre_x, (((0,), (0,)), ((), ())), preferred_element_type=F32)
    slab = width // n_col
    piece = slab // (ncore * nyl)
    w = w.reshape(ncore, nx, nyl, nyh, piece, width)
    w = lax.dynamic_index_in_dim(w, at["yh"], axis=3, keepdims=False)
    w = w.transpose(1, 2, 0, 3, 4).reshape(nx, slab, width)
    dpre_x = jnp.broadcast_to(dpre_x[None], (nx,) + dpre_x.shape)
    both = exchange(jnp.concatenate([dpre_x, w.astype(BF16)], axis=1), "x")
    dpre_all = both[:, : rows // nx].reshape(rows, width)
    w = both[:, rows // nx :].astype(F32).sum(0).astype(BF16)

    chunk = cols // n_row
    w = exchange(w.reshape(nyl * ncore, piece, width), ("yl", "core")).astype(F32).sum(0).astype(BF16)
    w_sum, output_x = lax.optimization_barrier((w, output_x))
    output = lax.dynamic_slice_in_dim(output_x, at["own_row"], own, axis=0)

    grad_in = lax.dot_general(
        dpre_all, weight, (((1,), (1,)), ((), ())), preferred_element_type=F32
    ).astype(BF16)
    partial_fg = lax.dot_general(masked, grad_in, (((0,), (0,)), ((), ())), preferred_element_type=F32)
    fg = partial_fg.astype(BF16).reshape(nz, nyl, ncore, chunk, width).transpose(2, 1, 0, 3, 4)
    fg, w_sum = lax.optimization_barrier((fg, w_sum))
    w = gather(w_sum, "z").astype(F32).sum(0) * (rows * n_row) ** (-0.5)
    w = w.astype(BF16)
    fg = halve(fg, "core", at)
    fg = halve(fg, "yl", at)
    fg, w, output = lax.optimization_barrier((fg, w, output))
    feature_grad = exchange(fg, "z").astype(F32).sum(0)

    for axis in ("yh", "yl"):
        w = lax.all_gather(w, axis, axis=0, tiled=True)
    w, feature_grad = lax.optimization_barrier((w, feature_grad))
    w = lax.all_gather(gather(w, "x").reshape(width // ncore, width), "core", axis=0, tiled=True)
    return (output, feature_grad, w.astype(F32).reshape(width, width))


def solution(mesh):
    fine = Mesh(mesh.devices.reshape(16, 2, 2, 4, 4), ("z", "yl", "core", "x", "yh"))
    row, col = ("z", "yl", "core"), ("x", "yh")
    return jax.shard_map(
        shards,
        mesh=fine,
        in_specs=(P(row, col), P(row, col), P(col + row, None), P(), P(row + col, None)),
        out_specs=(P(row + col, None), P(col + row, None), P()),
        check_vma=False,
    )
```
